256 devices in a mesh: section: 32 (over x, y, z_hi), expert: 8 (over z_lo, core).
Axes of the slice: x: 4, y: 4, z: 8 (z_hi: 2, z_lo: 4; z = z_hi * 4 + z_lo), core: 2. Of those that a mesh axis runs over, the one named last changes fastest.
Arguments:
- tokens_in: bfloat16 [8, 128, 2048], P(None, 'expert'), may hold values from -6 to 6
- expert_ids: int32 [32, 8, 128, 2], P('section'), may hold values from 0 to 7, all different within a row; in each aligned block of 16 rows (0 to 15, 16 to 31, ..., all dimensions but the last counted through in order) at most 5 rows name the same one
- router: bfloat16 [32, 2048, 8], P('section'), may hold values from -0.125 to 0.125
- norm_gain: float32 [32, 2048], P('section'), may hold values from 0.25 to 1.75
- w_gate: bfloat16 [32, 8, 2048, 512], P('section', 'expert'), may hold values from -0.125 to 0.125
- w_up: bfloat16 [32, 8, 2048, 512], P('section', 'expert'), may hold values from -0.125 to 0.125
- w_down: bfloat16 [32, 8, 512, 2048], P('section', 'expert'), may hold values from -0.25 to 0.25
Outputs:
- layer_states: float32 [32, 8, 128, 2048], P('section', None, 'expert')
The draws below stay inside these ranges and needn't reach their ends.
Inputs may be any that keep to these rules, and one draw needn't show every extreme that they name: `expert_ids`: each token names 2 different experts. Within one layer and micro-batch, each aligned block of 16 tokens (the rows of one device) names any one expert at most 5 times.
All inputs are finite; a program needn't handle non-finite values.
Results may differ from the reference program's by a relative error of at most 0.04.
Values may be sent and summed in bfloat16 or wider, within the bound.
No kernel may reach another device: no remote copies, remote signals or barrier semaphores. Data moves between devices by JAX's collectives and lax.ppermute only.
A program may use at most 64 MiB of HBM per device.

```python
import math
import jax
import jax.numpy as jnp
import numpy as np
from jax import lax

D = 2048
FF = 512
EXPERTS = 8
TOPK = 2
TOK_DEV = 16
MICRO = 8
TOKENS = 128
LAYERS = 32
CAP = 5


def steps_of(own_key, dims, cuts, smallest, high):
    loudness, own = 1.0, jax.random.fold_in(own_key, 6)
    for position, blocks in cuts:
        heights = jnp.exp(jax.random.uniform(jax.random.fold_in(own, position), (blocks,), jnp.float32, smallest / len(cuts), high / len(cuts)))
        loudness = loudness * jnp.repeat(heights, dims[position] // blocks).reshape([-1 if axis == position else 1 for axis in range(len(dims))])
    return loudness


def shared_out(stream_key, own, number, rows, number_of, top, limit, skew):
    sequence = jax.random.permutation(stream_key, number_of)
    crowded, usual = portions_of(number_of, rows * top, limit, skew, True), portions_of(number_of, rows * top, limit, skew, False)
    places = jnp.arange(number_of)

    def named(lengths, rotation):
        used = int((lengths > 0).sum())
        fixed = max(1, used // 4)
        shifted = fixed + (places - fixed + rotation * (used - fixed)) % max(1, number_of - fixed)
        return jnp.zeros((number_of,), jnp.int32).at[sequence[jnp.where(places < fixed, places, shifted)]].set(jnp.asarray(lengths, jnp.int32))

    lengths = jnp.where(number % 4 == 0, named(crowded, number // 4), named(usual, number - number // 4 - 1))
    mixed = jax.random.permutation(jax.random.fold_in(own, 3), number_of)
    source_of, receiver = mixed[0:number_of // 2 * 2:2], mixed[1:number_of // 2 * 2:2]
    margin = jnp.minimum(lengths[source_of] - 1, limit - lengths[receiver]) // 2
    margin = jnp.where((source_of == sequence[0]) | (receiver == sequence[0]) | (lengths[receiver] == 0), 0, jnp.maximum(margin, 0))
    shifted = jax.random.randint(jax.random.fold_in(own, 4), (number_of // 2,), 0, 1 << 20) % (margin + 1)
    lengths = lengths.at[source_of].add(-shifted).at[receiver].add(shifted)
    members = jnp.searchsorted(jnp.cumsum(lengths), jnp.arange(rows * top), side="right").astype(jnp.int32)
    listing = members.reshape(top, rows).T
    listing = listing[jax.random.permutation(jax.random.fold_in(own, 1), rows)]
    rotation = jax.random.randint(jax.random.fold_in(own, 2), (rows, 1), 0, top)
    return jnp.take_along_axis(listing, (jnp.arange(top)[None, :] + rotation) % top, axis=1)


def portions_of(number_of, total, bound, slope, full):
    portions = [(1 << 20) // math.isqrt(grade ** slope) + 1 for grade in range(1, number_of + 1)]
    largest = bound if full else min(bound, max(-(-total // number_of), total * portions[0] // sum(portions)))
    least = 1 if total - largest >= number_of - 1 else 0
    holding, spare = [largest] + [least] * (number_of - 1), total - largest - least * (number_of - 1)
    while spare > 0:
        movable = [i for i in range(1, number_of) if holding[i] < largest] or [i for i in range(1, number_of) if holding[i] < bound]
        whole, remaining = sum([portions[i] for i in movable]), spare
        for i in movable:
            addition = min(bound - holding[i], max(1, remaining * portions[i] // whole), spare)
            holding[i] = holding[i] + addition
            spare = spare - addition
    return np.array(holding)


def gaussian(stream_key, shape, scale, reach, cuts=(), kind=jnp.bfloat16):
    values = scale * jax.random.normal(stream_key, shape, jnp.float32)
    if cuts:
        values = values * steps_of(stream_key, shape, cuts, -0.22, 0.18)
    return jnp.clip(values, -reach, reach).astype(kind)


def setup_inputs(seed: int = 0) -> dict:
    seeds = jax.random.split(jax.random.key(seed), 8)
    tokens_in = gaussian(seeds[0], (MICRO, TOKENS, D), 1.0, 6.0, ((1, 8),))
    expert_ids_keys = jax.random.split(jax.random.fold_in(seeds[1], 1), LAYERS * MICRO * TOKENS // TOK_DEV)
    expert_ids_turns = jax.random.permutation(jax.random.fold_in(seeds[1], 3), LAYERS * MICRO * TOKENS // TOK_DEV)
    expert_ids = jax.vmap(lambda own, number: shared_out(jax.random.fold_in(seeds[1], 2), own, number, TOK_DEV, EXPERTS, TOPK, CAP, 1))(expert_ids_keys, expert_ids_turns).reshape((LAYERS, MICRO, TOKENS, TOPK))
    router = gaussian(seeds[2], (LAYERS, D, EXPERTS), D ** -0.5, 0.125, ((0, 32),))
    norm_gain = jnp.clip(1.0 + 0.15 * jax.random.normal(seeds[3], (LAYERS, D), jnp.float32), 0.25, 1.75)
    w_gate = gaussian(seeds[4], (LAYERS, EXPERTS, D, FF), D ** -0.5, 0.125, ((0, 32), (1, 8)))
    w_up = gaussian(seeds[5], (LAYERS, EXPERTS, D, FF), D ** -0.5, 0.125, ((0, 32), (1, 8)))
    w_down = gaussian(seeds[6], (LAYERS, EXPERTS, FF, D), FF ** -0.5, 0.25, ((0, 32), (1, 8)))
    return {"tokens_in": tokens_in, "expert_ids": expert_ids, "router": router, "norm_gain": norm_gain, "w_gate": w_gate, "w_up": w_up, "w_down": w_down}


norm_epsilon = 1e-06

def root_mean_norm(hidden, norm_scale):
    widened = hidden.astype(jnp.float32)
    mean_square = lax.optimization_barrier(jnp.mean(widened * widened, axis=-1, keepdims=True))
    return (widened * lax.rsqrt(mean_square + norm_epsilon) * norm_scale.astype(jnp.float32)).astype(jnp.bfloat16)

def expert_rows(row_block, gate_matrix, up_matrix, down_matrix):
    gate_part = jnp.dot(row_block, gate_matrix, preferred_element_type=jnp.float32)
    up_part = jnp.dot(row_block, up_matrix, preferred_element_type=jnp.float32)
    act = (jax.nn.silu(gate_part) * up_part).astype(jnp.bfloat16)
    return jnp.dot(act, down_matrix, preferred_element_type=jnp.float32).astype(jnp.bfloat16)

def reference(tokens_in, expert_ids, router, norm_gain, w_gate, w_up, w_down):
    micro_count, token_count, model_width = tokens_in.shape
    expert_total = w_gate.shape[1]
    top_count = expert_ids.shape[3]
    start_rows = tokens_in.reshape(micro_count * token_count, model_width).astype(jnp.float32)
    expert_range = jnp.arange(expert_total, dtype=jnp.int32)

    def apply_layer(hidden, layer_inputs):
        route_ids, router_matrix, norm_scale, gate_all, up_all, down_all = layer_inputs
        normed = root_mean_norm(hidden, norm_scale)
        logits = jnp.dot(normed, router_matrix, preferred_element_type=jnp.float32)
        flat_ids = route_ids.reshape(micro_count * token_count, top_count)
        picked = jnp.take_along_axis(logits, flat_ids, axis=1)
        scores = jax.nn.sigmoid(picked)
        gate_values = scores / lax.optimization_barrier(jnp.sum(scores, axis=1, keepdims=True))
        weight_table = lax.optimization_barrier(jnp.sum(gate_values[:, :, None] * (flat_ids[:, :, None] == expert_range[None, None, :]).astype(jnp.float32), axis=1))

        def add_expert(mixture, expert_inputs):
            gate_matrix, up_matrix, down_matrix, expert_index = expert_inputs
            expert_out = expert_rows(normed, gate_matrix, up_matrix, down_matrix)
            weights_column = lax.dynamic_index_in_dim(weight_table, expert_index, 1, keepdims=False)
            return (mixture + weights_column[:, None] * expert_out.astype(jnp.float32), None)
        mixture, _ = lax.scan(add_expert, jnp.zeros((micro_count * token_count, model_width), jnp.float32), (gate_all, up_all, down_all, expert_range))
        updated = hidden + mixture
        return (updated, updated)
    _, layer_outputs = lax.scan(apply_layer, start_rows, (expert_ids, router, norm_gain, w_gate, w_up, w_down))
    return layer_outputs.reshape(w_gate.shape[0], micro_count, token_count, model_width)
```

```python
import functools

import jax
import jax.numpy as jnp
from jax import lax
from jax.experimental import pallas as pl
from jax.experimental.pallas import tpu as pltpu
from jax.sharding import PartitionSpec as P

norm_epsilon = 1e-06
both = ("section", "expert")
z_size = 8
lanes = 128


def normed_of(hidden, norm_scale):
    mean_square = jnp.mean(hidden * hidden, axis=-1, keepdims=True)
    return (hidden * lax.rsqrt(mean_square + norm_epsilon) * norm_scale).astype(jnp.bfloat16)


def norm_kernel(hidden_ref, scale_ref, normed_ref):
    normed_ref[...] = normed_of(hidden_ref[...], scale_ref[...])


def add_norm_kernel(hidden_ref, own_ref, other_ref, scale_ref, sum_ref, normed_ref):
    total = hidden_ref[...] + (own_ref[...] + other_ref[...])
    sum_ref[...] = total
    normed_ref[...] = normed_of(total, scale_ref[...])


def add_kernel(hidden_ref, own_ref, other_ref, sum_ref):
    sum_ref[...] = hidden_ref[...] + (own_ref[...] + other_ref[...])


def experts_kernel(layer_half, place_ref, own_ref, other_ref, ids_ref, router_ref, *refs):
    kept, arrived = refs[:3], refs[3 : 3 + (z_size - 1) * 6]
    own_out, other_out, gates, ups, downs, rows, sems = refs[3 + (z_size - 1) * 6 :]
    active, my_z, my_core = place_ref[0], place_ref[1], place_ref[2]
    held = gates.shape[0]
    width, hidden_units = gates.shape[1:]
    own_rows = own_ref.shape[0]

    def halves_of(ref, *before):
        middle = ref.shape[len(before)] // 2
        return [ref.at[*before, pl.ds(0, middle)], ref.at[*before, pl.ds(middle, middle)]]

    def targets(i):
        return [half for ref in (gates, ups, downs) for half in halves_of(ref, i)]

    sources = [half for ref in kept for half in halves_of(ref)] + list(arrived)

    @pl.when(active == 1)
    def _():
        @pl.loop(0, held)
        def _(i):
            offset = lax.rem(my_z - (layer_half * held + i) + 2 * z_size, z_size)
            for r in range(z_size):

                @pl.when(offset == r)
                def _(r=r):
                    for m, target in enumerate(targets(i)):
                        pltpu.make_async_copy(sources[r * 6 + m], target, sems.at[i, m]).start()

        rows[pl.ds(0, own_rows)] = own_ref[...]
        rows[pl.ds(own_rows, own_rows)] = other_ref[...]
        logits = jnp.dot(rows[...], router_ref[...], preferred_element_type=jnp.float32)
        lane = lax.broadcasted_iota(jnp.int32, logits.shape, 1)
        first = lane == ids_ref[:, 0:1]
        second = lane == ids_ref[:, 1:2]
        zero = jnp.zeros_like(logits)
        score_first = jax.nn.sigmoid(jnp.sum(jnp.where(first, logits, zero), axis=1, keepdims=True))
        score_second = jax.nn.sigmoid(jnp.sum(jnp.where(second, logits, zero), axis=1, keepdims=True))
        score_sum = score_first + score_second
        table = jnp.where(first, score_first / score_sum, zero) + jnp.where(
            second, score_second / score_sum, zero
        )
        own_out[...] = jnp.zeros_like(own_out)
        other_out[...] = jnp.zeros_like(other_out)

        @pl.loop(0, held)
        def _(i):
            for m, target in enumerate(targets(i)):
                pltpu.make_async_copy(sources[m], target, sems.at[i, m]).wait()
            weight = jnp.sum(
                jnp.where(lane == 2 * i + my_core, table, zero), axis=1, keepdims=True
            )
            gate_part = jnp.dot(rows[...], gates[i], preferred_element_type=jnp.float32)
            up_part = jnp.dot(rows[...], ups[i], preferred_element_type=jnp.float32)
            act = (jax.nn.silu(gate_part) * up_part).astype(jnp.bfloat16)
            produced = jnp.dot(act, downs[i], preferred_element_type=jnp.float32)
            part = produced.astype(jnp.bfloat16).astype(jnp.float32) * weight
            own_out[...] += part[:own_rows]
            other_out[...] += part[own_rows:]


def vmem(count):
    return [pl.BlockSpec(memory_space=pltpu.VMEM)] * count


def run_norm(hidden, scale):
    return pl.pallas_call(
        norm_kernel,
        out_shape=jax.ShapeDtypeStruct(hidden.shape, jnp.bfloat16),
        in_specs=vmem(2),
        out_specs=vmem(1)[0],
    )(hidden, scale)


def run_add_norm(hidden, own, other, scale):
    return pl.pallas_call(
        add_norm_kernel,
        out_shape=(
            jax.ShapeDtypeStruct(hidden.shape, jnp.float32),
            jax.ShapeDtypeStruct(hidden.shape, jnp.bfloat16),
        ),
        in_specs=vmem(4),
        out_specs=tuple(vmem(2)),
    )(hidden, own, other, scale)


def run_add(hidden, own, other):
    return pl.pallas_call(
        add_kernel,
        out_shape=jax.ShapeDtypeStruct(hidden.shape, jnp.float32),
        in_specs=vmem(3),
        out_specs=vmem(1)[0],
    )(hidden, own, other)


def run_experts(layer_half, place, own, other, ids, router, sources):
    rows, width = own.shape
    units = sources[0].shape[1]
    held = z_size // 2
    return pl.pallas_call(
        functools.partial(experts_kernel, layer_half),
        out_shape=(jax.ShapeDtypeStruct(own.shape, jnp.float32),) * 2,
        in_specs=[pl.BlockSpec(memory_space=pltpu.SMEM)]
        + vmem(4)
        + [pl.BlockSpec(memory_space=pl.ANY)] * len(sources),
        out_specs=tuple(vmem(2)),
        scratch_shapes=[
            pltpu.VMEM((held, width, units), jnp.bfloat16),
            pltpu.VMEM((held, width, units), jnp.bfloat16),
            pltpu.VMEM((held, units, width), jnp.bfloat16),
            pltpu.VMEM((2 * rows, width), jnp.bfloat16),
            pltpu.SemaphoreType.DMA((held, 6)),
        ],
        compiler_params=pltpu.CompilerParams(vmem_limit_bytes=44 << 20),
    )(place, own, other, ids, router, *sources)


def device_at(ring, z, core):
    half = z_size // 2
    return (ring * 2 + z // half) * z_size + (z % half) * 2 + core


def around(rings, by):
    return [
        (device_at(ring, z, core), device_at(ring, (z + by) % z_size, core))
        for ring in range(rings)
        for z in range(z_size)
        for core in range(2)
    ]


def gather_ring(pieces, rings):
    forward, backward = around(rings, 1), around(rings, -1)
    slots = [[None] * len(pieces) for _ in range(z_size)]
    travelling = list(pieces)
    for step in range(1, z_size):
        for m in range(len(pieces)):
            travelling[m] = lax.ppermute(travelling[m], both, forward if m % 2 == 0 else backward)
            slots[step if m % 2 == 0 else z_size - step][m] = travelling[m]
    return [piece for slot in slots[1:] for piece in slot]


def shards(tokens_in, expert_ids, router, norm_gain, w_gate, w_up, w_down):
    sections = lax.axis_size("section")
    rings = sections // 2
    section_id = lax.axis_index("section")
    expert_id = lax.axis_index("expert")
    ring_id, upper = section_id // 2, section_id % 2
    my_z, my_core = upper * (z_size // 2) + expert_id // 2, expert_id % 2
    micro_count, tok_rows, width = tokens_in.shape
    own_micros = micro_count // 2
    row_count = own_micros * tok_rows
    other_core = [(e, e ^ 1) for e in range(z_size)]
    other_half = [(s, s ^ 1) for s in range(sections)]
    next_ring = [(s, s + 2) for s in range(sections - 2)]

    def halves(matrix):
        middle = matrix.shape[0] // 2
        return [matrix[:middle], matrix[middle:]]

    def both_layers(value):
        theirs = lax.ppermute(value, "section", other_half)
        return jnp.where(upper == 0, value, theirs), jnp.where(upper == 0, theirs, value)

    def rows_of(ids):
        mine = lax.dynamic_slice_in_dim(ids, upper * own_micros, own_micros, 0)
        blocks = [
            lax.dynamic_slice_in_dim(mine, block * tok_rows, tok_rows, 1)
            for block in (expert_id, expert_id ^ 1)
        ]
        return jnp.concatenate([b.reshape(row_count, -1) for b in blocks], axis=0)

    ids = [rows_of(layer) for layer in both_layers(expert_ids[0])]
    scales = both_layers(norm_gain)
    routers = [
        jnp.pad(layer, ((0, 0), (0, lanes - layer.shape[1]))) for layer in both_layers(router[0])
    ]
    matrices = [w_gate[0, 0], w_up[0, 0], w_down[0, 0]]
    sources = matrices + gather_ring([half for matrix in matrices for half in halves(matrix)], rings)
    entering = lax.dynamic_slice_in_dim(tokens_in, upper * own_micros, own_micros, 0)
    hidden = entering.reshape(row_count, width).astype(jnp.float32)

    def exchange(value):
        return lax.ppermute(value, "expert", other_core)

    def ring_step(step, state):
        hidden, stored_first, stored_second = state
        active = ring_id == step
        place = jnp.stack([active.astype(jnp.int32), my_z, my_core])
        normed = run_norm(hidden, scales[0])
        own, lent = run_experts(0, place, normed, exchange(normed), ids[0], routers[0], sources)
        middle, normed = run_add_norm(hidden, own, exchange(lent), scales[1])
        own, lent = run_experts(1, place, normed, exchange(normed), ids[1], routers[1], sources)
        leaving = run_add(middle, own, exchange(lent))
        stored_first = jnp.where(active, middle, stored_first)
        stored_second = jnp.where(active, leaving, stored_second)
        return lax.ppermute(leaving, "section", next_ring), stored_first, stored_second

    blank = jnp.zeros_like(hidden)
    _, stored_first, stored_second = lax.fori_loop(0, rings, ring_step, (hidden, blank, blank))
    kept = jnp.where(upper == 0, stored_first, stored_second)
    given = jnp.where(upper == 0, stored_second, stored_first)
    taken = lax.ppermute(given, "section", other_half)
    low = jnp.where(upper == 0, kept, taken)
    high = jnp.where(upper == 0, taken, kept)
    return jnp.concatenate([low, high], axis=0).reshape(1, micro_count, tok_rows, width)


def solution(mesh):
    return jax.shard_map(
        shards,
        mesh=mesh,
        in_specs=(
            P(None, "expert", None),
            P("section", None, None, None),
            P("section", None, None),
            P("section", None),
            P("section", "expert", None, None),
            P("section", "expert", None, None),
            P("section", "expert", None, None),
        ),
        out_specs=P("section", None, "expert", None),
        check_vma=False,
    )
```

```python
import functools

import jax
import jax.numpy as jnp
from jax import lax
from jax.experimental import pallas as pl
from jax.experimental.pallas import tpu as pltpu
from jax.sharding import PartitionSpec as P

norm_epsilon = 1e-06
both = ("section", "expert")
z_size = 8
source_count = 3 + (z_size - 1) * 6
lanes = 128


def normed_of(hidden, norm_scale):
    mean_square = jnp.mean(hidden * hidden, axis=-1, keepdims=True)
    return (hidden * lax.rsqrt(mean_square + norm_epsilon) * norm_scale).astype(jnp.bfloat16)


def layer_copies(layer_half, my_z, refs, loaded, sems):
    kept, arrived = refs[:3], refs[3:]
    held = z_size // 2

    def halves_of(ref, *before):
        middle = ref.shape[len(before)] // 2
        return [ref.at[*before, pl.ds(0, middle)], ref.at[*before, pl.ds(middle, middle)]]

    def targets(i):
        return [half for ref in loaded for half in halves_of(ref, i)]

    sources = [half for ref in kept for half in halves_of(ref)] + list(arrived)

    def start():
        @pl.loop(0, held)
        def _(i):
            offset = lax.rem(my_z - (layer_half * held + i) + 2 * z_size, z_size)
            for r in range(z_size):

                @pl.when(offset == r)
                def _(r=r):
                    for m, target in enumerate(targets(i)):
                        pltpu.make_async_copy(sources[r * 6 + m], target, sems.at[i, m]).start()

    def wait(i):
        for m, target in enumerate(targets(i)):
            pltpu.make_async_copy(sources[m], target, sems.at[i, m]).wait()

    return start, wait


def load_kernel(place_ref, *refs):
    sources, loaded, sems = refs[:source_count], refs[source_count:-1], refs[-1]
    start, wait = layer_copies(0, place_ref[1], sources, loaded, sems)

    @pl.when(place_ref[0] == 1)
    def _():
        start()
        pl.loop(0, z_size // 2)(wait)


def experts_sum(my_core, rows, ids_ref, router_ref, gates, ups, downs, total, wait=None):
    logits = jnp.dot(rows[...], router_ref[...], preferred_element_type=jnp.float32)
    lane = lax.broadcasted_iota(jnp.int32, logits.shape, 1)
    first = lane == ids_ref[:, 0:1]
    second = lane == ids_ref[:, 1:2]
    zero = jnp.zeros_like(logits)
    score_first = jax.nn.sigmoid(jnp.sum(jnp.where(first, logits, zero), axis=1, keepdims=True))
    score_second = jax.nn.sigmoid(jnp.sum(jnp.where(second, logits, zero), axis=1, keepdims=True))
    score_sum = score_first + score_second
    table = jnp.where(first, score_first / score_sum, zero) + jnp.where(
        second, score_second / score_sum, zero
    )
    total[...] = jnp.zeros_like(total)

    @pl.loop(0, gates.shape[0])
    def _(i):
        if wait is not None:
            wait(i)
        weight = jnp.sum(jnp.where(lane == 2 * i + my_core, table, zero), axis=1, keepdims=True)
        gate_part = jnp.dot(rows[...], gates[i], preferred_element_type=jnp.float32)
        up_part = jnp.dot(rows[...], ups[i], preferred_element_type=jnp.float32)
        act = (jax.nn.silu(gate_part) * up_part).astype(jnp.bfloat16)
        produced = jnp.dot(act, downs[i], preferred_element_type=jnp.float32)
        total[...] += produced.astype(jnp.bfloat16).astype(jnp.float32) * weight


def first_kernel(
    place_ref, mine_ref, other_ref, scale_ref, ids_ref, router_ref, gates, ups, downs,
    part_ref, lent_ref, rows,
):
    count = mine_ref.shape[0]

    @pl.when(place_ref[0] == 1)
    def _():
        rows[pl.ds(0, count)] = normed_of(mine_ref[...].astype(jnp.float32), scale_ref[...])
        rows[pl.ds(count, count)] = normed_of(other_ref[...].astype(jnp.float32), scale_ref[...])
        experts_sum(place_ref[2], rows, ids_ref, router_ref, gates, ups, downs, part_ref)
        lent_ref[...] = part_ref[...].astype(jnp.bfloat16)


def second_kernel(
    place_ref, mine_ref, other_ref, part_ref, back_ref, scale_ref, ids_ref, router_ref, stored_ref, *refs
):
    sources = refs[:source_count]
    middle_ref, own_ref, lent_ref, gates, ups, downs, rows, total, sems = refs[source_count:]
    count = mine_ref.shape[0]
    start, wait = layer_copies(1, place_ref[1], sources, (gates, ups, downs), sems)

    @pl.when(place_ref[0] == 1)
    def _():
        start()
        middle = mine_ref[...].astype(jnp.float32) + (
            part_ref[:count] + back_ref[count:].astype(jnp.float32)
        )
        middle_ref[...] = middle
        rows[pl.ds(0, count)] = normed_of(middle, scale_ref[...])
        beside = other_ref[...].astype(jnp.float32) + (
            part_ref[count:] + back_ref[:count].astype(jnp.float32)
        )
        rows[pl.ds(count, count)] = normed_of(beside, scale_ref[...])
        experts_sum(place_ref[2], rows, ids_ref, router_ref, gates, ups, downs, total, wait)
        own_ref[...] = total[:count]
        lent_ref[...] = total[count:].astype(jnp.bfloat16)

    @pl.when(place_ref[0] == 0)
    def _():
        middle_ref[...] = stored_ref[...]


def add_kernel(place_ref, middle_ref, own_ref, back_ref, stored_ref, sum_ref, sent_ref):
    @pl.when(place_ref[0] == 1)
    def _():
        total = middle_ref[...] + (own_ref[...] + back_ref[...].astype(jnp.float32))
        sum_ref[...] = total
        sent_ref[...] = total.astype(jnp.bfloat16)

    @pl.when(place_ref[0] == 0)
    def _():
        sum_ref[...] = stored_ref[...]


def vmem(count):
    return [pl.BlockSpec(memory_space=pltpu.VMEM)] * count


def like(shape, kind):
    return jax.ShapeDtypeStruct(shape, kind)


def layer_shapes(sources):
    width, units = sources[0].shape
    held = z_size // 2
    return [(held, width, units), (held, width, units), (held, units, width)]


def copy_sems():
    return pltpu.SemaphoreType.DMA((z_size // 2, 6))


def in_hbm(sources):
    return [pl.BlockSpec(memory_space=pltpu.HBM)] * len(sources)


def load_first(place, sources):
    width, units = sources[0].shape
    return pl.pallas_call(
        load_kernel,
        out_shape=tuple(pltpu.VMEM(shape, jnp.bfloat16) for shape in layer_shapes(sources)),
        in_specs=[pl.BlockSpec(memory_space=pltpu.SMEM)] + in_hbm(sources),
        out_specs=tuple(vmem(3)),
        scratch_shapes=[copy_sems()],
        compiler_params=pltpu.CompilerParams(vmem_limit_bytes=1 << 20),
        cost_estimate=pl.CostEstimate(
            flops=0, bytes_accessed=3 * z_size * width * units, transcendentals=0
        ),
    )(place, *sources)


def run_first(place, mine, other, scale, ids, router, weights):
    count, width = mine.shape
    return pl.pallas_call(
        first_kernel,
        out_shape=(like((2 * count, width), jnp.float32), like((2 * count, width), jnp.bfloat16)),
        in_specs=[pl.BlockSpec(memory_space=pltpu.SMEM)] + vmem(8),
        out_specs=tuple(vmem(2)),
        scratch_shapes=[pltpu.VMEM((2 * count, width), jnp.bfloat16)],
        compiler_params=pltpu.CompilerParams(vmem_limit_bytes=8 << 20),
    )(place, mine, other, scale, ids, router, *weights)


def run_second(place, mine, other, part, back, scale, ids, router, stored, sources):
    count, width = mine.shape
    return pl.pallas_call(
        second_kernel,
        out_shape=(
            like((count, width), jnp.float32),
            like((count, width), jnp.float32),
            like((count, width), jnp.bfloat16),
        ),
        in_specs=[pl.BlockSpec(memory_space=pltpu.SMEM)] + vmem(8) + in_hbm(sources),
        out_specs=tuple(vmem(3)),
        scratch_shapes=[pltpu.VMEM(shape, jnp.bfloat16) for shape in layer_shapes(sources)]
        + [
            pltpu.VMEM((2 * count, width), jnp.bfloat16),
            pltpu.VMEM((2 * count, width), jnp.float32),
            copy_sems(),
        ],
        input_output_aliases={8: 0},
        compiler_params=pltpu.CompilerParams(vmem_limit_bytes=34 << 20),
    )(place, mine, other, part, back, scale, ids, router, stored, *sources)


def run_add(place, middle, own, back, stored):
    return pl.pallas_call(
        add_kernel,
        out_shape=(like(middle.shape, jnp.float32), like(middle.shape, jnp.bfloat16)),
        in_specs=[pl.BlockSpec(memory_space=pltpu.SMEM)] + vmem(4),
        out_specs=tuple(vmem(2)),
        input_output_aliases={4: 0},
        compiler_params=pltpu.CompilerParams(vmem_limit_bytes=4 << 20),
    )(place, middle, own, back, stored)


def device_at(ring, z, core):
    half = z_size // 2
    return (ring * 2 + z // half) * z_size + (z % half) * 2 + core


def around(rings, by):
    return [
        (device_at(ring, z, core), device_at(ring, (z + by) % z_size, core))
        for ring in range(rings)
        for z in range(z_size)
        for core in range(2)
    ]


def gather_ring(pieces, rings):
    forward, backward = around(rings, 1), around(rings, -1)
    slots = [[None] * len(pieces) for _ in range(z_size)]
    travelling = list(pieces)
    for step in range(1, z_size):
        for m in range(len(pieces)):
            travelling[m] = lax.ppermute(travelling[m], both, forward if m % 2 == 0 else backward)
            slots[step if m % 2 == 0 else z_size - step][m] = travelling[m]
    return [piece for slot in slots[1:] for piece in slot]


def shards(tokens_in, expert_ids, router, norm_gain, w_gate, w_up, w_down):
    sections = lax.axis_size("section")
    rings = sections // 2
    section_id = lax.axis_index("section")
    expert_id = lax.axis_index("expert")
    ring_id, upper = section_id // 2, section_id % 2
    my_z, my_core = upper * (z_size // 2) + expert_id // 2, expert_id % 2
    micro_count, tok_rows, width = tokens_in.shape
    own_micros = micro_count // 2
    row_count = own_micros * tok_rows
    other_core = [(e, e ^ 1) for e in range(z_size)]
    other_half = [(s, s ^ 1) for s in range(sections)]
    next_ring = [(s, (s + 2) % sections) for s in range(sections)]

    def halves(matrix):
        middle = matrix.shape[0] // 2
        return [matrix[:middle], matrix[middle:]]

    def both_layers(value):
        theirs = lax.ppermute(value, "section", other_half)
        return jnp.where(upper == 0, value, theirs), jnp.where(upper == 0, theirs, value)

    def rows_of(ids):
        mine = lax.dynamic_slice_in_dim(ids, upper * own_micros, own_micros, 0)
        blocks = [
            lax.dynamic_slice_in_dim(mine, block * tok_rows, tok_rows, 1)
            for block in (expert_id, expert_id ^ 1)
        ]
        return jnp.concatenate([b.reshape(row_count, -1) for b in blocks], axis=0)

    ids = [rows_of(layer) for layer in both_layers(expert_ids[0])]
    scales = both_layers(norm_gain)
    routers = [
        jnp.pad(layer, ((0, 0), (0, lanes - layer.shape[1]))) for layer in both_layers(router[0])
    ]
    matrices = [w_gate[0, 0], w_up[0, 0], w_down[0, 0]]
    sources = matrices + gather_ring([half for matrix in matrices for half in halves(matrix)], rings)
    entering = lax.dynamic_slice_in_dim(tokens_in, upper * own_micros, own_micros, 0)
    entering = entering.reshape(row_count, width)

    def exchange(value):
        return lax.ppermute(value, "expert", other_core)

    def ring_step(step, state):
        sent, stored_first, stored_second = state
        place = jnp.stack([(ring_id == step).astype(jnp.int32), my_z, my_core])
        mine = lax.ppermute(sent, "section", next_ring)
        mine, weights = lax.optimization_barrier((mine, load_first(place, sources)))
        other = exchange(mine)
        part, lent = run_first(place, mine, other, scales[0], ids[0], routers[0], weights)
        back = exchange(lent)
        stored_first, own, lent = run_second(
            place, mine, other, part, back, scales[1], ids[1], routers[1], stored_first, sources
        )
        back = exchange(lent)
        stored_second, sent = run_add(place, stored_first, own, back, stored_second)
        return sent, stored_first, stored_second

    blank = jnp.zeros(entering.shape, jnp.float32)
    _, stored_first, stored_second = lax.fori_loop(0, rings, ring_step, (entering, blank, blank))
    kept = jnp.where(upper == 0, stored_first, stored_second)
    given = jnp.where(upper == 0, stored_second, stored_first)
    taken = lax.ppermute(given.astype(jnp.bfloat16), "section", other_half).astype(jnp.float32)
    low = jnp.where(upper == 0, kept, taken)
    high = jnp.where(upper == 0, taken, kept)
    return jnp.concatenate([low, high], axis=0).reshape(1, micro_count, tok_rows, width)


def solution(mesh):
    return jax.shard_map(
        shards,
        mesh=mesh,
        in_specs=(
            P(None, "expert", None),
            P("section", None, None, None),
            P("section", None, None),
            P("section", None),
            P("section", "expert", None, None),
            P("section", "expert", None, None),
            P("section", "expert", None, None),
        ),
        out_specs=P("section", None, "expert", None),
        check_vma=False,
    )
```

```python
import functools

import jax
import jax.numpy as jnp
from jax import lax
from jax.experimental import pallas as pl
from jax.experimental.pallas import tpu as pltpu
from jax.sharding import PartitionSpec as P

norm_epsilon = 1e-06
both = ("section", "expert")
z_size = 8
source_count = 3 + (z_size - 1) * 6
early = 3
ready_count = 3 if early else 0
lanes = 128


def normed_of(hidden, norm_scale):
    mean_square = jnp.mean(hidden * hidden, axis=-1, keepdims=True)
    return (hidden * lax.rsqrt(mean_square + norm_epsilon) * norm_scale).astype(jnp.bfloat16)


def layer_copies(layer_half, experts, my_z, refs, loaded, sems):
    kept, arrived = refs[:3], refs[3:]
    first, count = experts

    def halves_of(ref, *before):
        middle = ref.shape[len(before)] // 2
        return [ref.at[*before, pl.ds(0, middle)], ref.at[*before, pl.ds(middle, middle)]]

    def targets(i):
        return [half for ref in loaded for half in halves_of(ref, i)]

    sources = [half for ref in kept for half in halves_of(ref)] + list(arrived)

    def start():
        @pl.loop(0, count)
        def _(i):
            owner = layer_half * (z_size // 2) + first + i
            offset = lax.rem(my_z - owner + 2 * z_size, z_size)
            for r in range(z_size):

                @pl.when(offset == r)
                def _(r=r):
                    for m, target in enumerate(targets(i)):
                        pltpu.make_async_copy(sources[r * 6 + m], target, sems.at[i, m]).start()

    def wait(i):
        for m, target in enumerate(targets(i)):
            pltpu.make_async_copy(sources[m], target, sems.at[i, m]).wait()

    return start, wait


def load_kernel(place_ref, *refs):
    sources, (middle_ref, last_ref) = refs[:source_count], refs[source_count : source_count + 2]
    loaded, (first_out, second_out) = refs[source_count + 4 : -5], refs[-5:-3]
    first_sems, second_sems, out_sems = refs[-3:]
    held = z_size // 2
    copies = [layer_copies(0, (0, held), place_ref[1], sources, loaded[:3], first_sems)]
    if early:
        copies.append(layer_copies(1, (0, early), place_ref[1], sources, loaded[3:], second_sems))

    @pl.when(place_ref[0] == 1)
    def _():
        for start, _ in copies:
            start()
        for (_, wait), count in zip(copies, (held, early)):
            pl.loop(0, count)(wait)

    @pl.when(place_ref[3] == 1)
    def _():
        away = [
            pltpu.make_async_copy(middle_ref, first_out, out_sems.at[0]),
            pltpu.make_async_copy(last_ref, second_out, out_sems.at[1]),
        ]
        for copy in away:
            copy.start()
        for copy in away:
            copy.wait()


def experts_sum(my_core, rows, ids_ref, router_ref, experts, total):
    logits = jnp.dot(rows[...], router_ref[...], preferred_element_type=jnp.float32)
    lane = lax.broadcasted_iota(jnp.int32, logits.shape, 1)
    first = lane == ids_ref[:, 0:1]
    second = lane == ids_ref[:, 1:2]
    zero = jnp.zeros_like(logits)
    score_first = jax.nn.sigmoid(jnp.sum(jnp.where(first, logits, zero), axis=1, keepdims=True))
    score_second = jax.nn.sigmoid(jnp.sum(jnp.where(second, logits, zero), axis=1, keepdims=True))
    score_sum = score_first + score_second
    table = jnp.where(first, score_first / score_sum, zero) + jnp.where(
        second, score_second / score_sum, zero
    )
    for i, (gates, ups, downs, wait) in enumerate(experts):
        wait()
        weight = jnp.sum(jnp.where(lane == 2 * i + my_core, table, zero), axis=1, keepdims=True)
        gate_part = jnp.dot(rows[...], gates[...], preferred_element_type=jnp.float32)
        up_part = jnp.dot(rows[...], ups[...], preferred_element_type=jnp.float32)
        act = (jax.nn.silu(gate_part) * up_part).astype(jnp.bfloat16)
        produced = jnp.dot(act, downs[...], preferred_element_type=jnp.float32)
        part = produced.astype(jnp.bfloat16).astype(jnp.float32) * weight
        if i == 0:
            total[...] = part
        else:
            total[...] += part


def at_once(refs):
    return [tuple(ref.at[i] for ref in refs) + (lambda: None,) for i in range(refs[0].shape[0])]


def first_kernel(
    place_ref, mine_ref, other_ref, scale_ref, ids_ref, router_ref, gates, ups, downs,
    part_ref, lent_ref, rows,
):
    count = mine_ref.shape[0]

    @pl.when(place_ref[0] == 1)
    def _():
        rows[pl.ds(0, count)] = normed_of(mine_ref[...].astype(jnp.float32), scale_ref[...])
        rows[pl.ds(count, count)] = normed_of(other_ref[...].astype(jnp.float32), scale_ref[...])
        experts = at_once((gates, ups, downs))
        experts_sum(place_ref[2], rows, ids_ref, router_ref, experts, part_ref)
        lent_ref[...] = part_ref[...].astype(jnp.bfloat16)


def second_kernel(
    place_ref, mine_ref, other_ref, part_ref, back_ref, scale_ref, ids_ref, router_ref, *refs
):
    ready, sources, refs = refs[:ready_count], refs[ready_count:][:source_count], refs[ready_count + source_count :]
    middle_ref, own_ref, lent_ref, gates, ups, downs, rows, total, sems = refs
    count, late = mine_ref.shape[0], gates.shape[0]
    start, wait = layer_copies(
        1, (early, late), place_ref[1], sources, (gates, ups, downs), sems
    )

    @pl.when(place_ref[0] == 1)
    def _():
        start()
        middle = mine_ref[...].astype(jnp.float32) + (
            part_ref[:count] + back_ref[count:].astype(jnp.float32)
        )
        middle_ref[...] = middle
        rows[pl.ds(0, count)] = normed_of(middle, scale_ref[...])
        beside = other_ref[...].astype(jnp.float32) + (
            part_ref[count:] + back_ref[:count].astype(jnp.float32)
        )
        rows[pl.ds(count, count)] = normed_of(beside, scale_ref[...])
        experts = (at_once(ready) if early else []) + [
            (gates.at[i], ups.at[i], downs.at[i], functools.partial(wait, i)) for i in range(late)
        ]
        experts_sum(place_ref[2], rows, ids_ref, router_ref, experts, total)
        own_ref[...] = total[:count]
        lent_ref[...] = total[count:].astype(jnp.bfloat16)


def add_kernel(place_ref, middle_ref, own_ref, back_ref, sum_ref, sent_ref):
    @pl.when(place_ref[0] == 1)
    def _():
        total = middle_ref[...] + (own_ref[...] + back_ref[...].astype(jnp.float32))
        sum_ref[...] = total
        sent_ref[...] = total.astype(jnp.bfloat16)


def vmem(count):
    return [pl.BlockSpec(memory_space=pltpu.VMEM)] * count


def like(shape, kind):
    return jax.ShapeDtypeStruct(shape, kind)


def layer_shapes(sources, count):
    width, units = sources[0].shape
    return [(count, width, units), (count, width, units), (count, units, width)]


def copy_sems(count):
    return pltpu.SemaphoreType.DMA((max(count, 1), 6))


def in_hbm(count):
    return [pl.BlockSpec(memory_space=pltpu.HBM)] * count


def load_ahead(place, sources, middle, last, stored):
    width, units = sources[0].shape
    held = z_size // 2
    shapes = layer_shapes(sources, held) + (layer_shapes(sources, early) if early else [])
    results = pl.pallas_call(
        load_kernel,
        out_shape=tuple(pltpu.VMEM(shape, jnp.bfloat16) for shape in shapes)
        + tuple(like(array.shape, array.dtype) for array in stored),
        in_specs=[pl.BlockSpec(memory_space=pltpu.SMEM)]
        + in_hbm(len(sources))
        + [pl.BlockSpec(memory_space=pl.ANY)] * 2
        + in_hbm(2),
        out_specs=tuple(vmem(len(shapes)) + in_hbm(2)),
        scratch_shapes=[copy_sems(held), copy_sems(early), pltpu.SemaphoreType.DMA((2,))],
        input_output_aliases={source_count + 3 + i: len(shapes) + i for i in range(2)},
        compiler_params=pltpu.CompilerParams(vmem_limit_bytes=1 << 20),
        cost_estimate=pl.CostEstimate(
            flops=0, bytes_accessed=6 * (held + early) * width * units, transcendentals=0
        ),
    )(place, *sources, middle, last, *stored)
    return results[:3], results[3:-2], results[-2:]


def run_first(place, mine, other, scale, ids, router, weights):
    count, width = mine.shape
    return pl.pallas_call(
        first_kernel,
        out_shape=(like((2 * count, width), jnp.float32), like((2 * count, width), jnp.bfloat16)),
        in_specs=[pl.BlockSpec(memory_space=pltpu.SMEM)] + vmem(8),
        out_specs=tuple(vmem(2)),
        scratch_shapes=[pltpu.VMEM((2 * count, width), jnp.bfloat16)],
        compiler_params=pltpu.CompilerParams(vmem_limit_bytes=8 << 20),
    )(place, mine, other, scale, ids, router, *weights)


def run_second(place, mine, other, part, back, scale, ids, router, ready, sources):
    count, width = mine.shape
    return pl.pallas_call(
        second_kernel,
        out_shape=(
            like((count, width), jnp.float32),
            like((count, width), jnp.float32),
            like((count, width), jnp.bfloat16),
        ),
        in_specs=[pl.BlockSpec(memory_space=pltpu.SMEM)]
        + vmem(7 + len(ready))
        + in_hbm(len(sources)),
        out_specs=tuple(vmem(3)),
        scratch_shapes=[
            pltpu.VMEM(shape, jnp.bfloat16) for shape in layer_shapes(sources, z_size // 2 - early)
        ]
        + [
            pltpu.VMEM((2 * count, width), jnp.bfloat16),
            pltpu.VMEM((2 * count, width), jnp.float32),
            copy_sems(z_size // 2 - early),
        ],
        compiler_params=pltpu.CompilerParams(
            vmem_limit_bytes=(10 + 6 * (z_size // 2 - early)) << 20
        ),
    )(place, mine, other, part, back, scale, ids, router, *ready, *sources)


def run_add(place, middle, own, back):
    return pl.pallas_call(
        add_kernel,
        out_shape=(like(middle.shape, jnp.float32), like(middle.shape, jnp.bfloat16)),
        in_specs=[pl.BlockSpec(memory_space=pltpu.SMEM)] + vmem(3),
        out_specs=tuple(vmem(2)),
        compiler_params=pltpu.CompilerParams(vmem_limit_bytes=4 << 20),
    )(place, middle, own, back)


def device_at(ring, z, core):
    half = z_size // 2
    return (ring * 2 + z // half) * z_size + (z % half) * 2 + core


def around(rings, by):
    return [
        (device_at(ring, z, core), device_at(ring, (z + by) % z_size, core))
        for ring in range(rings)
        for z in range(z_size)
        for core in range(2)
    ]


def gather_ring(pieces, rings):
    forward, backward = around(rings, 1), around(rings, -1)
    slots = [[None] * len(pieces) for _ in range(z_size)]
    travelling = list(pieces)
    for step in range(1, z_size):
        for m in range(len(pieces)):
            travelling[m] = lax.ppermute(travelling[m], both, forward if m % 2 == 0 else backward)
            slots[step if m % 2 == 0 else z_size - step][m] = travelling[m]
    return [piece for slot in slots[1:] for piece in slot]


def shards(tokens_in, expert_ids, router, norm_gain, w_gate, w_up, w_down):
    sections = lax.axis_size("section")
    rings = sections // 2
    section_id = lax.axis_index("section")
    expert_id = lax.axis_index("expert")
    ring_id, upper = section_id // 2, section_id % 2
    my_z, my_core = upper * (z_size // 2) + expert_id // 2, expert_id % 2
    micro_count, tok_rows, width = tokens_in.shape
    own_micros = micro_count // 2
    row_count = own_micros * tok_rows
    other_core = [(e, e ^ 1) for e in range(z_size)]
    other_half = [(s, s ^ 1) for s in range(sections)]
    next_ring = [(s, (s + 2) % sections) for s in range(sections)]

    def halves(matrix):
        middle = matrix.shape[0] // 2
        return [matrix[:middle], matrix[middle:]]

    def both_layers(value):
        theirs = lax.ppermute(value, "section", other_half)
        return jnp.where(upper == 0, value, theirs), jnp.where(upper == 0, theirs, value)

    def rows_of(ids):
        mine = lax.dynamic_slice_in_dim(ids, upper * own_micros, own_micros, 0)
        blocks = [
            lax.dynamic_slice_in_dim(mine, block * tok_rows, tok_rows, 1)
            for block in (expert_id, expert_id ^ 1)
        ]
        return jnp.concatenate([b.reshape(row_count, -1) for b in blocks], axis=0)

    ids = [rows_of(layer) for layer in both_layers(expert_ids[0])]
    scales = both_layers(norm_gain)
    routers = [
        jnp.pad(layer, ((0, 0), (0, lanes - layer.shape[1]))) for layer in both_layers(router[0])
    ]
    matrices = [w_gate[0, 0], w_up[0, 0], w_down[0, 0]]
    sources = matrices + gather_ring([half for matrix in matrices for half in halves(matrix)], rings)
    entering = lax.dynamic_slice_in_dim(tokens_in, upper * own_micros, own_micros, 0)
    entering = entering.reshape(row_count, width)

    def exchange(value):
        return lax.ppermute(value, "expert", other_core)

    def ring_step(step, state):
        sent, middle, last, stored = state
        flags = [(ring_id == step).astype(jnp.int32), my_z, my_core]
        place = jnp.stack(flags + [(ring_id == step - 1).astype(jnp.int32)])
        mine = lax.ppermute(sent, "section", next_ring)
        ahead = load_ahead(place, sources, middle, last, stored)
        mine, (weights, ready, stored) = lax.optimization_barrier((mine, ahead))
        other = exchange(mine)
        part, lent = run_first(place, mine, other, scales[0], ids[0], routers[0], weights)
        back = exchange(lent)
        middle, own, lent = run_second(
            place, mine, other, part, back, scales[1], ids[1], routers[1], ready, sources
        )
        last, sent = run_add(place, middle, own, exchange(lent))
        return sent, middle, last, stored

    blank = jnp.zeros(entering.shape, jnp.float32)
    state = (entering, blank, blank, (blank, blank + 0))
    _, middle, last, stored = lax.fori_loop(0, rings, ring_step, state)
    final = ring_id == rings - 1
    stored_first = jnp.where(final, middle, stored[0])
    stored_second = jnp.where(final, last, stored[1])
    kept = jnp.where(upper == 0, stored_first, stored_second)
    given = jnp.where(upper == 0, stored_second, stored_first)
    taken = lax.ppermute(given.astype(jnp.bfloat16), "section", other_half).astype(jnp.float32)
    low = jnp.where(upper == 0, kept, taken)
    high = jnp.where(upper == 0, taken, kept)
    return jnp.concatenate([low, high], axis=0).reshape(1, micro_count, tok_rows, width)


def solution(mesh):
    return jax.shard_map(
        shards,
        mesh=mesh,
        in_specs=(
            P(None, "expert", None),
            P("section", None, None, None),
            P("section", None, None),
            P("section", None),
            P("section", "expert", None, None),
            P("section", "expert", None, None),
            P("section", "expert", None, None),
        ),
        out_specs=P("section", None, "expert", None),
        check_vma=False,
    )
```

```python
import functools

import jax
import jax.numpy as jnp
from jax import lax
from jax.experimental import pallas as pl
from jax.experimental.pallas import tpu as pltpu
from jax.sharding import PartitionSpec as P

norm_epsilon = 1e-06
both = ("section", "expert")
z_size = 8
source_count = 3 + (z_size - 1) * 6
early = 2
ready_count = 3 if early else 0
lanes = 128


def normed_of(hidden, norm_scale):
    mean_square = jnp.mean(hidden * hidden, axis=-1, keepdims=True)
    return (hidden * lax.rsqrt(mean_square + norm_epsilon) * norm_scale).astype(jnp.bfloat16)


def layer_copies(layer_half, experts, my_z, refs, loaded, sems):
    kept, arrived = refs[:3], refs[3:]
    first, count = experts

    def halves_of(ref, *before):
        middle = ref.shape[len(before)] // 2
        return [ref.at[*before, pl.ds(0, middle)], ref.at[*before, pl.ds(middle, middle)]]

    def targets(i):
        return [half for ref in loaded for half in halves_of(ref, i)]

    sources = [half for ref in kept for half in halves_of(ref)] + list(arrived)

    def start():
        @pl.loop(0, count)
        def _(i):
            owner = layer_half * (z_size // 2) + first + i
            offset = lax.rem(my_z - owner + 2 * z_size, z_size)
            for r in range(z_size):

                @pl.when(offset == r)
                def _(r=r):
                    for m, target in enumerate(targets(i)):
                        pltpu.make_async_copy(sources[r * 6 + m], target, sems.at[i, m]).start()

    def wait(i):
        for m, target in enumerate(targets(i)):
            pltpu.make_async_copy(sources[m], target, sems.at[i, m]).wait()

    return start, wait


def load_kernel(place_ref, *refs):
    sources, (middle_ref, last_ref) = refs[:source_count], refs[source_count : source_count + 2]
    loaded, (first_out, second_out) = refs[source_count + 4 : -5], refs[-5:-3]
    first_sems, second_sems, out_sems = refs[-3:]
    held = z_size // 2
    copies = [layer_copies(0, (0, held), place_ref[1], sources, loaded[:3], first_sems)]
    if early:
        copies.append(layer_copies(1, (0, early), place_ref[1], sources, loaded[3:], second_sems))

    @pl.when(place_ref[0] == 1)
    def _():
        for start, _ in copies:
            start()
        for (_, wait), count in zip(copies, (held, early)):
            pl.loop(0, count)(wait)

    @pl.when(place_ref[3] == 1)
    def _():
        away = [
            pltpu.make_async_copy(middle_ref, first_out, out_sems.at[0]),
            pltpu.make_async_copy(last_ref, second_out, out_sems.at[1]),
        ]
        for copy in away:
            copy.start()
        for copy in away:
            copy.wait()


def experts_sum(my_core, rows, ids_ref, router_ref, experts, total):
    logits = jnp.dot(rows[...], router_ref[...], preferred_element_type=jnp.float32)
    lane = lax.broadcasted_iota(jnp.int32, logits.shape, 1)
    first = lane == ids_ref[:, 0:1]
    second = lane == ids_ref[:, 1:2]
    zero = jnp.zeros_like(logits)
    score_first = jax.nn.sigmoid(jnp.sum(jnp.where(first, logits, zero), axis=1, keepdims=True))
    score_second = jax.nn.sigmoid(jnp.sum(jnp.where(second, logits, zero), axis=1, keepdims=True))
    score_sum = score_first + score_second
    table = jnp.where(first, score_first / score_sum, zero) + jnp.where(
        second, score_second / score_sum, zero
    )
    for i, (gates, ups, downs, wait) in enumerate(experts):
        wait()
        weight = jnp.sum(jnp.where(lane == 2 * i + my_core, table, zero), axis=1, keepdims=True)
        gate_part = jnp.dot(rows[...], gates[...], preferred_element_type=jnp.float32)
        up_part = jnp.dot(rows[...], ups[...], preferred_element_type=jnp.float32)
        act = (jax.nn.silu(gate_part) * up_part).astype(jnp.bfloat16)
        produced = jnp.dot(act, downs[...], preferred_element_type=jnp.float32)
        part = produced.astype(jnp.bfloat16).astype(jnp.float32) * weight
        if i == 0:
            total[...] = part
        else:
            total[...] += part


def at_once(refs):
    return [tuple(ref.at[i] for ref in refs) + (lambda: None,) for i in range(refs[0].shape[0])]


def first_kernel(
    place_ref, mine_ref, other_ref, scale_ref, ids_ref, router_ref, gates, ups, downs,
    part_ref, lent_ref, rows,
):
    count = mine_ref.shape[0]

    @pl.when(place_ref[0] == 1)
    def _():
        rows[pl.ds(0, count)] = normed_of(mine_ref[...].astype(jnp.float32), scale_ref[...])
        rows[pl.ds(count, count)] = normed_of(other_ref[...].astype(jnp.float32), scale_ref[...])
        experts = at_once((gates, ups, downs))
        experts_sum(place_ref[2], rows, ids_ref, router_ref, experts, part_ref)
        lent_ref[...] = part_ref[...].astype(jnp.bfloat16)


def second_kernel(
    place_ref, mine_ref, other_ref, part_ref, back_ref, scale_ref, ids_ref, router_ref, *refs
):
    ready, sources, refs = refs[:ready_count], refs[ready_count:][:source_count], refs[ready_count + source_count :]
    middle_ref, own_ref, lent_ref, gates, ups, downs, rows, total, sems = refs
    count, late = mine_ref.shape[0], gates.shape[0]
    start, wait = layer_copies(
        1, (early, late), place_ref[1], sources, (gates, ups, downs), sems
    )

    @pl.when(place_ref[0] == 1)
    def _():
        start()
        middle = mine_ref[...].astype(jnp.float32) + (
            part_ref[:count] + back_ref[count:].astype(jnp.float32)
        )
        middle_ref[...] = middle
        rows[pl.ds(0, count)] = normed_of(middle, scale_ref[...])
        beside = other_ref[...].astype(jnp.float32) + (
            part_ref[count:] + back_ref[:count].astype(jnp.float32)
        )
        rows[pl.ds(count, count)] = normed_of(beside, scale_ref[...])
        experts = (at_once(ready) if early else []) + [
            (gates.at[i], ups.at[i], downs.at[i], functools.partial(wait, i)) for i in range(late)
        ]
        experts_sum(place_ref[2], rows, ids_ref, router_ref, experts, total)
        own_ref[...] = total[:count]
        lent_ref[...] = total[count:].astype(jnp.bfloat16)


def add_kernel(place_ref, middle_ref, own_ref, back_ref, sum_ref, sent_ref):
    @pl.when(place_ref[0] == 1)
    def _():
        total = middle_ref[...] + (own_ref[...] + back_ref[...].astype(jnp.float32))
        sum_ref[...] = total
        sent_ref[...] = total.astype(jnp.bfloat16)


def vmem(count):
    return [pl.BlockSpec(memory_space=pltpu.VMEM)] * count


def like(shape, kind):
    return jax.ShapeDtypeStruct(shape, kind)


def layer_shapes(sources, count):
    width, units = sources[0].shape
    return [(count, width, units), (count, width, units), (count, units, width)]


def copy_sems(count):
    return pltpu.SemaphoreType.DMA((max(count, 1), 6))


def in_hbm(count):
    return [pl.BlockSpec(memory_space=pltpu.HBM)] * count


def load_ahead(place, sources, middle, last, stored):
    width, units = sources[0].shape
    held = z_size // 2
    shapes = layer_shapes(sources, held) + (layer_shapes(sources, early) if early else [])
    results = pl.pallas_call(
        load_kernel,
        out_shape=tuple(pltpu.VMEM(shape, jnp.bfloat16) for shape in shapes)
        + tuple(like(array.shape, array.dtype) for array in stored),
        in_specs=[pl.BlockSpec(memory_space=pltpu.SMEM)]
        + in_hbm(len(sources))
        + vmem(2)
        + in_hbm(2),
        out_specs=tuple(vmem(len(shapes)) + in_hbm(2)),
        scratch_shapes=[copy_sems(held), copy_sems(early), pltpu.SemaphoreType.DMA((2,))],
        input_output_aliases={source_count + 3 + i: len(shapes) + i for i in range(2)},
        compiler_params=pltpu.CompilerParams(vmem_limit_bytes=3 << 20),
        cost_estimate=pl.CostEstimate(
            flops=0, bytes_accessed=6 * (held + early) * width * units, transcendentals=0
        ),
    )(place, *sources, middle, last, *stored)
    return results[:3], results[3:-2], results[-2:]


def run_first(place, mine, other, scale, ids, router, weights):
    count, width = mine.shape
    return pl.pallas_call(
        first_kernel,
        out_shape=(like((2 * count, width), jnp.float32), like((2 * count, width), jnp.bfloat16)),
        in_specs=[pl.BlockSpec(memory_space=pltpu.SMEM)] + vmem(8),
        out_specs=tuple(vmem(2)),
        scratch_shapes=[pltpu.VMEM((2 * count, width), jnp.bfloat16)],
        compiler_params=pltpu.CompilerParams(vmem_limit_bytes=8 << 20),
    )(place, mine, other, scale, ids, router, *weights)


def run_second(place, mine, other, part, back, scale, ids, router, ready, sources):
    count, width = mine.shape
    return pl.pallas_call(
        second_kernel,
        out_shape=(
            like((count, width), jnp.float32),
            like((count, width), jnp.float32),
            like((count, width), jnp.bfloat16),
        ),
        in_specs=[pl.BlockSpec(memory_space=pltpu.SMEM)]
        + vmem(7 + len(ready))
        + in_hbm(len(sources)),
        out_specs=tuple(vmem(3)),
        scratch_shapes=[
            pltpu.VMEM(shape, jnp.bfloat16) for shape in layer_shapes(sources, z_size // 2 - early)
        ]
        + [
            pltpu.VMEM((2 * count, width), jnp.bfloat16),
            pltpu.VMEM((2 * count, width), jnp.float32),
            copy_sems(z_size // 2 - early),
        ],
        compiler_params=pltpu.CompilerParams(
            vmem_limit_bytes=(10 + 6 * (z_size // 2 - early)) << 20
        ),
    )(place, mine, other, part, back, scale, ids, router, *ready, *sources)


def run_add(place, middle, own, back):
    return pl.pallas_call(
        add_kernel,
        out_shape=(like(middle.shape, jnp.float32), like(middle.shape, jnp.bfloat16)),
        in_specs=[pl.BlockSpec(memory_space=pltpu.SMEM)] + vmem(3),
        out_specs=tuple(vmem(2)),
        compiler_params=pltpu.CompilerParams(vmem_limit_bytes=4 << 20),
    )(place, middle, own, back)


def device_at(ring, z, core):
    half = z_size // 2
    return (ring * 2 + z // half) * z_size + (z % half) * 2 + core


def around(rings, by):
    return [
        (device_at(ring, z, core), device_at(ring, (z + by) % z_size, core))
        for ring in range(rings)
        for z in range(z_size)
        for core in range(2)
    ]


def gather_ring(pieces, rings):
    forward, backward = around(rings, 1), around(rings, -1)
    slots = [[None] * len(pieces) for _ in range(z_size)]
    travelling = list(pieces)
    for step in range(1, z_size):
        for m in range(0, len(pieces), 2):
            pair = lax.optimization_barrier((travelling[m], travelling[m + 1]))
            travelling[m] = lax.ppermute(pair[0], both, forward)
            travelling[m + 1] = lax.ppermute(pair[1], both, backward)
            slots[step][m], slots[z_size - step][m + 1] = travelling[m], travelling[m + 1]
    return [piece for slot in slots[1:] for piece in slot]


def shards(tokens_in, expert_ids, router, norm_gain, w_gate, w_up, w_down):
    sections = lax.axis_size("section")
    rings = sections // 2
    section_id = lax.axis_index("section")
    expert_id = lax.axis_index("expert")
    ring_id, upper = section_id // 2, section_id % 2
    my_z, my_core = upper * (z_size // 2) + expert_id // 2, expert_id % 2
    micro_count, tok_rows, width = tokens_in.shape
    own_micros = micro_count // 2
    row_count = own_micros * tok_rows
    other_core = [(e, e ^ 1) for e in range(z_size)]
    other_half = [(s, s ^ 1) for s in range(sections)]
    next_ring = [(s, (s + 2) % sections) for s in range(sections)]

    def halves(matrix):
        middle = matrix.shape[0] // 2
        return [matrix[:middle], matrix[middle:]]

    def both_layers(value):
        theirs = lax.ppermute(value, "section", other_half)
        return jnp.where(upper == 0, value, theirs), jnp.where(upper == 0, theirs, value)

    def rows_of(ids):
        mine = lax.dynamic_slice_in_dim(ids, upper * own_micros, own_micros, 0)
        blocks = [
            lax.dynamic_slice_in_dim(mine, block * tok_rows, tok_rows, 1)
            for block in (expert_id, expert_id ^ 1)
        ]
        return jnp.concatenate([b.reshape(row_count, -1) for b in blocks], axis=0)

    matrices = [w_gate[0, 0], w_up[0, 0], w_down[0, 0]]
    sources = matrices + gather_ring([half for matrix in matrices for half in halves(matrix)], rings)
    small = lax.optimization_barrier((expert_ids[0], norm_gain, router[0], sources[3 + 6]))
    ids = [rows_of(layer) for layer in both_layers(small[0])]
    scales = both_layers(small[1])
    routers = [
        jnp.pad(layer, ((0, 0), (0, lanes - layer.shape[1]))) for layer in both_layers(small[2])
    ]
    entering = lax.dynamic_slice_in_dim(tokens_in, upper * own_micros, own_micros, 0)
    entering = entering.reshape(row_count, width)

    def exchange(value):
        return lax.ppermute(value, "expert", other_core)

    def ring_step(step, state):
        sent, middle, last, stored = state
        flags = [(ring_id == step).astype(jnp.int32), my_z, my_core]
        place = jnp.stack(flags + [(ring_id == step - 1).astype(jnp.int32)])
        mine = lax.ppermute(sent, "section", next_ring)
        ahead = load_ahead(place, sources, middle, last, stored)
        mine, (weights, ready, stored) = lax.optimization_barrier((mine, ahead))
        other = exchange(mine)
        part, lent = run_first(place, mine, other, scales[0], ids[0], routers[0], weights)
        back = exchange(lent)
        middle, own, lent = run_second(
            place, mine, other, part, back, scales[1], ids[1], routers[1], ready, sources
        )
        last, sent = run_add(place, middle, own, exchange(lent))
        return sent, middle, last, stored

    blank = jnp.zeros(entering.shape, jnp.float32)
    state = (entering, blank, blank, (blank, blank + 0))
    _, middle, last, stored = lax.fori_loop(0, rings, ring_step, state)
    final = ring_id == rings - 1
    stored_first = jnp.where(final, middle, stored[0])
    stored_second = jnp.where(final, last, stored[1])
    kept = jnp.where(upper == 0, stored_first, stored_second)
    given = jnp.where(upper == 0, stored_second, stored_first)
    taken = lax.ppermute(given.astype(jnp.bfloat16), "section", other_half).astype(jnp.float32)
    low = jnp.where(upper == 0, kept, taken)
    high = jnp.where(upper == 0, taken, kept)
    return jnp.concatenate([low, high], axis=0).reshape(1, micro_count, tok_rows, width)


def solution(mesh):
    return jax.shard_map(
        shards,
        mesh=mesh,
        in_specs=(
            P(None, "expert", None),
            P("section", None, None, None),
            P("section", None, None),
            P("section", None),
            P("section", "expert", None, None),
            P("section", "expert", None, None),
            P("section", "expert", None, None),
        ),
        out_specs=P("section", None, "expert", None),
        check_vma=False,
    )
```

```python
import functools

import jax
import jax.numpy as jnp
from jax import lax
from jax.experimental import pallas as pl
from jax.experimental.pallas import tpu as pltpu
from jax.sharding import PartitionSpec as P

norm_epsilon = 1e-06
both = ("section", "expert")
z_size = 8
source_count = 3 + (z_size - 1) * 6
early = 2
ready_count = 3 if early else 0
lanes = 128


def normed_of(hidden, norm_scale):
    mean_square = jnp.mean(hidden * hidden, axis=-1, keepdims=True)
    return (hidden * lax.rsqrt(mean_square + norm_epsilon) * norm_scale).astype(jnp.bfloat16)


def layer_copies(layer_half, experts, my_z, refs, loaded, sems):
    kept, arrived = refs[:3], refs[3:]
    first, count = experts

    def halves_of(ref, *before):
        middle = ref.shape[len(before)] // 2
        return [ref.at[*before, pl.ds(0, middle)], ref.at[*before, pl.ds(middle, middle)]]

    def targets(i):
        return [half for ref in loaded for half in halves_of(ref, i)]

    sources = [half for ref in kept for half in halves_of(ref)] + list(arrived)

    def start():
        @pl.loop(0, count)
        def _(i):
            owner = layer_half * (z_size // 2) + first + i
            offset = lax.rem(my_z - owner + 2 * z_size, z_size)
            for r in range(z_size):

                @pl.when(offset == r)
                def _(r=r):
                    for m, target in enumerate(targets(i)):
                        pltpu.make_async_copy(sources[r * 6 + m], target, sems.at[i, m]).start()

    def wait(i):
        for m, target in enumerate(targets(i)):
            pltpu.make_async_copy(sources[m], target, sems.at[i, m]).wait()

    return start, wait


def load_kernel(place_ref, *refs):
    sources, (middle_ref, base_ref, back_ref) = refs[:source_count], refs[source_count:][:3]
    loaded, (first_out, second_out) = refs[source_count + 5 : -6], refs[-6:-4]
    leaving, first_sems, second_sems, out_sems = refs[-4:]
    held = z_size // 2
    copies = [layer_copies(0, (0, held), place_ref[1], sources, loaded[:3], first_sems)]
    if early:
        copies.append(layer_copies(1, (0, early), place_ref[1], sources, loaded[3:], second_sems))

    @pl.when(place_ref[0] == 1)
    def _():
        for start, _ in copies:
            start()
        for (_, wait), count in zip(copies, (held, early)):
            pl.loop(0, count)(wait)

    @pl.when(place_ref[3] == 1)
    def _():
        leaving[...] = base_ref[...] + back_ref[...].astype(jnp.float32)
        away = [
            pltpu.make_async_copy(middle_ref, first_out, out_sems.at[0]),
            pltpu.make_async_copy(leaving, second_out, out_sems.at[1]),
        ]
        for copy in away:
            copy.start()
        for copy in away:
            copy.wait()


def experts_sum(my_core, rows, ids_ref, router_ref, experts, total):
    logits = jnp.dot(rows[...], router_ref[...], preferred_element_type=jnp.float32)
    lane = lax.broadcasted_iota(jnp.int32, logits.shape, 1)
    first = lane == ids_ref[:, 0:1]
    second = lane == ids_ref[:, 1:2]
    zero = jnp.zeros_like(logits)
    score_first = jax.nn.sigmoid(jnp.sum(jnp.where(first, logits, zero), axis=1, keepdims=True))
    score_second = jax.nn.sigmoid(jnp.sum(jnp.where(second, logits, zero), axis=1, keepdims=True))
    score_sum = score_first + score_second
    table = jnp.where(first, score_first / score_sum, zero) + jnp.where(
        second, score_second / score_sum, zero
    )
    for i, (gates, ups, downs, wait) in enumerate(experts):
        wait()
        weight = jnp.sum(jnp.where(lane == 2 * i + my_core, table, zero), axis=1, keepdims=True)
        gate_part = jnp.dot(rows[...], gates[...], preferred_element_type=jnp.float32)
        up_part = jnp.dot(rows[...], ups[...], preferred_element_type=jnp.float32)
        act = (jax.nn.silu(gate_part) * up_part).astype(jnp.bfloat16)
        produced = jnp.dot(act, downs[...], preferred_element_type=jnp.float32)
        part = produced.astype(jnp.bfloat16).astype(jnp.float32) * weight
        if i == 0:
            total[...] = part
        else:
            total[...] += part


def at_once(refs):
    return [tuple(ref.at[i] for ref in refs) + (lambda: None,) for i in range(refs[0].shape[0])]


def first_kernel(
    place_ref, mine_ref, other_ref, scale_ref, ids_ref, router_ref, gates, ups, downs,
    part_ref, lent_ref, rows,
):
    count = mine_ref.shape[0]

    @pl.when(place_ref[0] == 1)
    def _():
        rows[pl.ds(0, count)] = normed_of(mine_ref[...].astype(jnp.float32), scale_ref[...])
        rows[pl.ds(count, count)] = normed_of(other_ref[...].astype(jnp.float32), scale_ref[...])
        experts = at_once((gates, ups, downs))
        experts_sum(place_ref[2], rows, ids_ref, router_ref, experts, part_ref)
        lent_ref[...] = part_ref[...].astype(jnp.bfloat16)


def second_kernel(
    place_ref, mine_ref, other_ref, part_ref, back_ref, scale_ref, ids_ref, router_ref, *refs
):
    ready, sources, refs = refs[:ready_count], refs[ready_count:][:source_count], refs[ready_count + source_count :]
    middle_out, base_ref, lent_ref, gates, ups, downs, middle_ref, rows, total, sems, out_sem = refs
    count, late = mine_ref.shape[0], gates.shape[0]
    start, wait = layer_copies(
        1, (early, late), place_ref[1], sources, (gates, ups, downs), sems
    )

    @pl.when(place_ref[0] == 1)
    def _():
        start()
        middle = mine_ref[...].astype(jnp.float32) + (
            part_ref[:count] + back_ref[count:].astype(jnp.float32)
        )
        middle_ref[...] = middle
        put_away = pltpu.make_async_copy(middle_ref, middle_out, out_sem)
        put_away.start()
        rows[pl.ds(0, count)] = normed_of(middle, scale_ref[...])
        beside = other_ref[...].astype(jnp.float32) + (
            part_ref[count:] + back_ref[:count].astype(jnp.float32)
        )
        rows[pl.ds(count, count)] = normed_of(beside, scale_ref[...])
        experts = (at_once(ready) if early else []) + [
            (gates.at[i], ups.at[i], downs.at[i], functools.partial(wait, i)) for i in range(late)
        ]
        experts_sum(place_ref[2], rows, ids_ref, router_ref, experts, total)
        base_ref[...] = middle_ref[...] + total[:count]
        lent_ref[...] = total[count:].astype(jnp.bfloat16)
        put_away.wait()


def add_kernel(base_ref, back_ref, sent_ref):
    sent_ref[...] = (base_ref[...] + back_ref[...].astype(jnp.float32)).astype(jnp.bfloat16)


def vmem(count):
    return [pl.BlockSpec(memory_space=pltpu.VMEM)] * count


def like(shape, kind):
    return jax.ShapeDtypeStruct(shape, kind)


def layer_shapes(sources, count):
    width, units = sources[0].shape
    return [(count, width, units), (count, width, units), (count, units, width)]


def copy_sems(count):
    return pltpu.SemaphoreType.DMA((max(count, 1), 6))


def in_hbm(count):
    return [pl.BlockSpec(memory_space=pltpu.HBM)] * count


def load_ahead(place, sources, middle, base, back, stored):
    width, units = sources[0].shape
    held = z_size // 2
    shapes = layer_shapes(sources, held) + (layer_shapes(sources, early) if early else [])
    results = pl.pallas_call(
        load_kernel,
        out_shape=tuple(pltpu.VMEM(shape, jnp.bfloat16) for shape in shapes)
        + tuple(like(array.shape, array.dtype) for array in stored),
        in_specs=[pl.BlockSpec(memory_space=pltpu.SMEM)]
        + in_hbm(len(sources))
        + vmem(3)
        + in_hbm(2),
        out_specs=tuple(vmem(len(shapes)) + in_hbm(2)),
        scratch_shapes=[
            pltpu.VMEM(base.shape, jnp.float32),
            copy_sems(held),
            copy_sems(early),
            pltpu.SemaphoreType.DMA((2,)),
        ],
        input_output_aliases={source_count + 4 + i: len(shapes) + i for i in range(2)},
        compiler_params=pltpu.CompilerParams(vmem_limit_bytes=3 << 20),
        cost_estimate=pl.CostEstimate(
            flops=0, bytes_accessed=6 * (held + early) * width * units, transcendentals=0
        ),
    )(place, *sources, middle, base, back, *stored)
    return results[:3], results[3:-2], results[-2:]


def run_first(place, mine, other, scale, ids, router, weights):
    count, width = mine.shape
    return pl.pallas_call(
        first_kernel,
        out_shape=(like((2 * count, width), jnp.float32), like((2 * count, width), jnp.bfloat16)),
        in_specs=[pl.BlockSpec(memory_space=pltpu.SMEM)] + vmem(8),
        out_specs=tuple(vmem(2)),
        scratch_shapes=[pltpu.VMEM((2 * count, width), jnp.bfloat16)],
        compiler_params=pltpu.CompilerParams(vmem_limit_bytes=8 << 20),
    )(place, mine, other, scale, ids, router, *weights)


def run_second(place, mine, other, part, back, scale, ids, router, ready, sources):
    count, width = mine.shape
    return pl.pallas_call(
        second_kernel,
        out_shape=(
            like((count, width), jnp.float32),
            like((count, width), jnp.float32),
            like((count, width), jnp.bfloat16),
        ),
        in_specs=[pl.BlockSpec(memory_space=pltpu.SMEM)]
        + vmem(7 + len(ready))
        + in_hbm(len(sources)),
        out_specs=tuple(in_hbm(1) + vmem(2)),
        scratch_shapes=[
            pltpu.VMEM(shape, jnp.bfloat16) for shape in layer_shapes(sources, z_size // 2 - early)
        ]
        + [
            pltpu.VMEM((count, width), jnp.float32),
            pltpu.VMEM((2 * count, width), jnp.bfloat16),
            pltpu.VMEM((2 * count, width), jnp.float32),
            copy_sems(z_size // 2 - early),
            pltpu.SemaphoreType.DMA(()),
        ],
        compiler_params=pltpu.CompilerParams(
            vmem_limit_bytes=(10 + 6 * (z_size // 2 - early)) << 20
        ),
    )(place, mine, other, part, back, scale, ids, router, *ready, *sources)


def run_add(base, back):
    return pl.pallas_call(
        add_kernel,
        out_shape=like(base.shape, jnp.bfloat16),
        in_specs=vmem(2),
        out_specs=vmem(1)[0],
        compiler_params=pltpu.CompilerParams(vmem_limit_bytes=3 << 20),
    )(base, back)


def device_at(ring, z, core):
    half = z_size // 2
    return (ring * 2 + z // half) * z_size + (z % half) * 2 + core


def around(rings, by):
    return [
        (device_at(ring, z, core), device_at(ring, (z + by) % z_size, core))
        for ring in range(rings)
        for z in range(z_size)
        for core in range(2)
    ]


def gather_ring(pieces, rings):
    forward, backward = around(rings, 1), around(rings, -1)
    slots = [[None] * len(pieces) for _ in range(z_size)]
    travelling = list(pieces)
    for step in range(1, z_size):
        for m in range(0, len(pieces), 2):
            pair = lax.optimization_barrier((travelling[m], travelling[m + 1]))
            travelling[m] = lax.ppermute(pair[0], both, forward)
            travelling[m + 1] = lax.ppermute(pair[1], both, backward)
            slots[step][m], slots[z_size - step][m + 1] = travelling[m], travelling[m + 1]
    return [piece for slot in slots[1:] for piece in slot]


def shards(tokens_in, expert_ids, router, norm_gain, w_gate, w_up, w_down):
    sections = lax.axis_size("section")
    rings = sections // 2
    section_id = lax.axis_index("section")
    expert_id = lax.axis_index("expert")
    ring_id, upper = section_id // 2, section_id % 2
    my_z, my_core = upper * (z_size // 2) + expert_id // 2, expert_id % 2
    micro_count, tok_rows, width = tokens_in.shape
    own_micros = micro_count // 2
    row_count = own_micros * tok_rows
    other_core = [(e, e ^ 1) for e in range(z_size)]
    other_half = [(s, s ^ 1) for s in range(sections)]
    next_ring = [(s, (s + 2) % sections) for s in range(sections)]

    def halves(matrix):
        middle = matrix.shape[0] // 2
        return [matrix[:middle], matrix[middle:]]

    def both_layers(value):
        theirs = lax.ppermute(value, "section", other_half)
        return jnp.where(upper == 0, value, theirs), jnp.where(upper == 0, theirs, value)

    def rows_of(ids):
        mine = lax.dynamic_slice_in_dim(ids, upper * own_micros, own_micros, 0)
        blocks = [
            lax.dynamic_slice_in_dim(mine, block * tok_rows, tok_rows, 1)
            for block in (expert_id, expert_id ^ 1)
        ]
        return jnp.concatenate([b.reshape(row_count, -1) for b in blocks], axis=0)

    matrices = [w_gate[0, 0], w_up[0, 0], w_down[0, 0]]
    sources = matrices + gather_ring([half for matrix in matrices for half in halves(matrix)], rings)
    small = lax.optimization_barrier((expert_ids[0], norm_gain, router[0], sources[3 + 6]))
    ids = [rows_of(layer) for layer in both_layers(small[0])]
    scales = both_layers(small[1])
    routers = [
        jnp.pad(layer, ((0, 0), (0, lanes - layer.shape[1]))) for layer in both_layers(small[2])
    ]
    entering = lax.dynamic_slice_in_dim(tokens_in, upper * own_micros, own_micros, 0)
    entering = entering.reshape(row_count, width)

    def exchange(value):
        return lax.ppermute(value, "expert", other_core)

    def ring_step(step, state):
        sent, middle, base, back, stored = state
        flags = [(ring_id == step).astype(jnp.int32), my_z, my_core]
        place = jnp.stack(flags + [(ring_id == step - 1).astype(jnp.int32)])
        mine = lax.ppermute(sent, "section", next_ring)
        ahead = load_ahead(place, sources, middle, base, back, stored)
        mine, (weights, ready, stored) = lax.optimization_barrier((mine, ahead))
        other = exchange(mine)
        part, lent = run_first(place, mine, other, scales[0], ids[0], routers[0], weights)
        back = exchange(lent)
        middle, base, lent = run_second(
            place, mine, other, part, back, scales[1], ids[1], routers[1], ready, sources
        )
        back = exchange(lent)
        return run_add(base, back), middle, base, back, stored

    blank = jnp.zeros(entering.shape, jnp.float32)
    state = (entering, blank, blank, entering, (blank, blank + 0))
    _, middle, base, back, stored = lax.fori_loop(0, rings, ring_step, state)
    final = ring_id == rings - 1
    stored_first = jnp.where(final, middle, stored[0])
    stored_second = jnp.where(final, base + back.astype(jnp.float32), stored[1])
    kept = jnp.where(upper == 0, stored_first, stored_second)
    given = jnp.where(upper == 0, stored_second, stored_first)
    taken = lax.ppermute(given.astype(jnp.bfloat16), "section", other_half).astype(jnp.float32)
    low = jnp.where(upper == 0, kept, taken)
    high = jnp.where(upper == 0, taken, kept)
    return jnp.concatenate([low, high], axis=0).reshape(1, micro_count, tok_rows, width)


def solution(mesh):
    return jax.shard_map(
        shards,
        mesh=mesh,
        in_specs=(
            P(None, "expert", None),
            P("section", None, None, None),
            P("section", None, None),
            P("section", None),
            P("section", "expert", None, None),
            P("section", "expert", None, None),
            P("section", "expert", None, None),
        ),
        out_specs=P("section", None, "expert", None),
        check_vma=False,
    )
```

```python
import functools

import jax
import jax.numpy as jnp
from jax import lax
from jax.experimental import pallas as pl
from jax.experimental.pallas import tpu as pltpu
from jax.sharding import PartitionSpec as P

norm_epsilon = 1e-06
both = ("section", "expert")
z_size = 8
source_count = 3 + (z_size - 1) * 6
early = 2
ready_count = 3 if early else 0
lanes = 128


def normed_of(hidden, norm_scale):
    mean_square = jnp.mean(hidden * hidden, axis=-1, keepdims=True)
    return (hidden * lax.rsqrt(mean_square + norm_epsilon) * norm_scale).astype(jnp.bfloat16)


def layer_copies(layer_half, experts, my_z, refs, loaded, sems):
    kept, arrived = refs[:3], refs[3:]
    first, count = experts

    def halves_of(ref, *before):
        middle = ref.shape[len(before)] // 2
        return [ref.at[*before, pl.ds(0, middle)], ref.at[*before, pl.ds(middle, middle)]]

    def targets(i):
        return [half for ref in loaded for half in halves_of(ref, i)]

    sources = [half for ref in kept for half in halves_of(ref)] + list(arrived)

    def start():
        @pl.loop(0, count)
        def _(i):
            owner = layer_half * (z_size // 2) + first + i
            offset = lax.rem(my_z - owner + 2 * z_size, z_size)
            for r in range(z_size):

                @pl.when(offset == r)
                def _(r=r):
                    for m, target in enumerate(targets(i)):
                        pltpu.make_async_copy(sources[r * 6 + m], target, sems.at[i, m]).start()

    def wait(i):
        for m, target in enumerate(targets(i)):
            pltpu.make_async_copy(sources[m], target, sems.at[i, m]).wait()

    return start, wait


def load_kernel(place_ref, *refs):
    sources, (middle_ref, base_ref, back_ref) = refs[:source_count], refs[source_count:][:3]
    loaded, (first_out, second_out) = refs[source_count + 5 : -6], refs[-6:-4]
    leaving, first_sems, second_sems, out_sems = refs[-4:]
    held = z_size // 2
    copies = [layer_copies(0, (0, held), place_ref[1], sources, loaded[:3], first_sems)]
    if early:
        copies.append(layer_copies(1, (0, early), place_ref[1], sources, loaded[3:], second_sems))

    @pl.when(place_ref[0] == 1)
    def _():
        for start, _ in copies:
            start()
        for (_, wait), count in zip(copies, (held, early)):
            pl.loop(0, count)(wait)

    @pl.when(place_ref[3] == 1)
    def _():
        leaving[...] = base_ref[...] + back_ref[...].astype(jnp.float32)
        away = [
            pltpu.make_async_copy(middle_ref, first_out, out_sems.at[0]),
            pltpu.make_async_copy(leaving, second_out, out_sems.at[1]),
        ]
        for copy in away:
            copy.start()
        for copy in away:
            copy.wait()


def experts_sum(my_core, rows, ids_ref, router_ref, experts, total):
    logits = jnp.dot(rows[...], router_ref[...], preferred_element_type=jnp.float32)
    lane = lax.broadcasted_iota(jnp.int32, logits.shape, 1)
    first = lane == ids_ref[:, 0:1]
    second = lane == ids_ref[:, 1:2]
    zero = jnp.zeros_like(logits)
    score_first = jax.nn.sigmoid(jnp.sum(jnp.where(first, logits, zero), axis=1, keepdims=True))
    score_second = jax.nn.sigmoid(jnp.sum(jnp.where(second, logits, zero), axis=1, keepdims=True))
    score_sum = score_first + score_second
    table = jnp.where(first, score_first / score_sum, zero) + jnp.where(
        second, score_second / score_sum, zero
    )
    for i, (gates, ups, downs, wait) in enumerate(experts):
        wait()
        weight = jnp.sum(jnp.where(lane == 2 * i + my_core, table, zero), axis=1, keepdims=True)
        gate_part = jnp.dot(rows[...], gates[...], preferred_element_type=jnp.float32)
        up_part = jnp.dot(rows[...], ups[...], preferred_element_type=jnp.float32)
        act = (jax.nn.silu(gate_part) * up_part).astype(jnp.bfloat16)
        produced = jnp.dot(act, downs[...], preferred_element_type=jnp.float32)
        part = produced.astype(jnp.bfloat16).astype(jnp.float32) * weight
        if i == 0:
            total[...] = part
        else:
            total[...] += part


def at_once(refs):
    return [tuple(ref.at[i] for ref in refs) + (lambda: None,) for i in range(refs[0].shape[0])]


def first_kernel(
    place_ref, mine_ref, other_ref, scale_ref, ids_ref, router_ref, gates, ups, downs,
    part_ref, lent_ref, rows,
):
    count = mine_ref.shape[0]

    @pl.when(place_ref[0] == 1)
    def _():
        rows[pl.ds(0, count)] = normed_of(mine_ref[...].astype(jnp.float32), scale_ref[...])
        rows[pl.ds(count, count)] = normed_of(other_ref[...].astype(jnp.float32), scale_ref[...])
        experts = at_once((gates, ups, downs))
        experts_sum(place_ref[2], rows, ids_ref, router_ref, experts, part_ref)
        lent_ref[...] = part_ref[...].astype(jnp.bfloat16)


def second_kernel(
    place_ref, mine_ref, other_ref, part_ref, back_ref, scale_ref, ids_ref, router_ref, *refs
):
    ready, sources, refs = refs[:ready_count], refs[ready_count:][:source_count], refs[ready_count + source_count :]
    middle_out, base_ref, lent_ref, gates, ups, downs, middle_ref, rows, total, sems, out_sem = refs
    count, late = mine_ref.shape[0], gates.shape[0]
    start, wait = layer_copies(
        1, (early, late), place_ref[1], sources, (gates, ups, downs), sems
    )

    @pl.when(place_ref[0] == 1)
    def _():
        start()
        middle = mine_ref[...].astype(jnp.float32) + (
            part_ref[:count] + back_ref[count:].astype(jnp.float32)
        )
        middle_ref[...] = middle
        put_away = pltpu.make_async_copy(middle_ref, middle_out, out_sem)
        put_away.start()
        rows[pl.ds(0, count)] = normed_of(middle, scale_ref[...])
        beside = other_ref[...].astype(jnp.float32) + (
            part_ref[count:] + back_ref[:count].astype(jnp.float32)
        )
        rows[pl.ds(count, count)] = normed_of(beside, scale_ref[...])
        experts = (at_once(ready) if early else []) + [
            (gates.at[i], ups.at[i], downs.at[i], functools.partial(wait, i)) for i in range(late)
        ]
        experts_sum(place_ref[2], rows, ids_ref, router_ref, experts, total)
        base_ref[...] = middle_ref[...] + total[:count]
        lent_ref[...] = total[count:].astype(jnp.bfloat16)
        put_away.wait()


def vmem(count):
    return [pl.BlockSpec(memory_space=pltpu.VMEM)] * count


def like(shape, kind):
    return jax.ShapeDtypeStruct(shape, kind)


def layer_shapes(sources, count):
    width, units = sources[0].shape
    return [(count, width, units), (count, width, units), (count, units, width)]


def copy_sems(count):
    return pltpu.SemaphoreType.DMA((max(count, 1), 6))


def in_hbm(count):
    return [pl.BlockSpec(memory_space=pltpu.HBM)] * count


def load_ahead(place, sources, middle, base, back, stored):
    width, units = sources[0].shape
    held = z_size // 2
    shapes = layer_shapes(sources, held) + (layer_shapes(sources, early) if early else [])
    results = pl.pallas_call(
        load_kernel,
        out_shape=tuple(pltpu.VMEM(shape, jnp.bfloat16) for shape in shapes)
        + tuple(like(array.shape, array.dtype) for array in stored),
        in_specs=[pl.BlockSpec(memory_space=pltpu.SMEM)]
        + in_hbm(len(sources))
        + vmem(3)
        + in_hbm(2),
        out_specs=tuple(vmem(len(shapes)) + in_hbm(2)),
        scratch_shapes=[
            pltpu.VMEM(base.shape, jnp.float32),
            copy_sems(held),
            copy_sems(early),
            pltpu.SemaphoreType.DMA((2,)),
        ],
        input_output_aliases={source_count + 4 + i: len(shapes) + i for i in range(2)},
        compiler_params=pltpu.CompilerParams(vmem_limit_bytes=3 << 20),
        cost_estimate=pl.CostEstimate(
            flops=0, bytes_accessed=6 * (held + early) * width * units, transcendentals=0
        ),
    )(place, *sources, middle, base, back, *stored)
    return results[:3], results[3:-2], results[-2:]


def run_first(place, mine, other, scale, ids, router, weights):
    count, width = mine.shape
    return pl.pallas_call(
        first_kernel,
        out_shape=(like((2 * count, width), jnp.float32), like((2 * count, width), jnp.bfloat16)),
        in_specs=[pl.BlockSpec(memory_space=pltpu.SMEM)] + vmem(8),
        out_specs=tuple(vmem(2)),
        scratch_shapes=[pltpu.VMEM((2 * count, width), jnp.bfloat16)],
        compiler_params=pltpu.CompilerParams(vmem_limit_bytes=8 << 20),
    )(place, mine, other, scale, ids, router, *weights)


def run_second(place, mine, other, part, back, scale, ids, router, ready, sources):
    count, width = mine.shape
    return pl.pallas_call(
        second_kernel,
        out_shape=(
            like((count, width), jnp.float32),
            like((count, width), jnp.float32),
            like((count, width), jnp.bfloat16),
        ),
        in_specs=[pl.BlockSpec(memory_space=pltpu.SMEM)]
        + vmem(7 + len(ready))
        + in_hbm(len(sources)),
        out_specs=tuple(in_hbm(1) + vmem(2)),
        scratch_shapes=[
            pltpu.VMEM(shape, jnp.bfloat16) for shape in layer_shapes(sources, z_size // 2 - early)
        ]
        + [
            pltpu.VMEM((count, width), jnp.float32),
            pltpu.VMEM((2 * count, width), jnp.bfloat16),
            pltpu.VMEM((2 * count, width), jnp.float32),
            copy_sems(z_size // 2 - early),
            pltpu.SemaphoreType.DMA(()),
        ],
        compiler_params=pltpu.CompilerParams(
            vmem_limit_bytes=(10 + 6 * (z_size // 2 - early)) << 20
        ),
    )(place, mine, other, part, back, scale, ids, router, *ready, *sources)


def device_at(ring, z, core):
    half = z_size // 2
    return (ring * 2 + z // half) * z_size + (z % half) * 2 + core


def around(rings, by):
    return [
        (device_at(ring, z, core), device_at(ring, (z + by) % z_size, core))
        for ring in range(rings)
        for z in range(z_size)
        for core in range(2)
    ]


def gather_ring(pieces, rings):
    forward, backward = around(rings, 1), around(rings, -1)
    slots = [[None] * len(pieces) for _ in range(z_size)]
    travelling = list(pieces)
    for step in range(1, z_size):
        for m in range(0, len(pieces), 2):
            pair = lax.optimization_barrier((travelling[m], travelling[m + 1]))
            travelling[m] = lax.ppermute(pair[0], both, forward)
            travelling[m + 1] = lax.ppermute(pair[1], both, backward)
            slots[step][m], slots[z_size - step][m + 1] = travelling[m], travelling[m + 1]
    return [piece for slot in slots[1:] for piece in slot]


def shards(tokens_in, expert_ids, router, norm_gain, w_gate, w_up, w_down):
    sections = lax.axis_size("section")
    rings = sections // 2
    section_id = lax.axis_index("section")
    expert_id = lax.axis_index("expert")
    ring_id, upper = section_id // 2, section_id % 2
    my_z, my_core = upper * (z_size // 2) + expert_id // 2, expert_id % 2
    micro_count, tok_rows, width = tokens_in.shape
    own_micros = micro_count // 2
    row_count = own_micros * tok_rows
    other_core = [(e, e ^ 1) for e in range(z_size)]
    other_half = [(s, s ^ 1) for s in range(sections)]
    next_ring = [(s, (s + 2) % sections) for s in range(sections)]

    def halves(matrix):
        middle = matrix.shape[0] // 2
        return [matrix[:middle], matrix[middle:]]

    def both_layers(value):
        theirs = lax.ppermute(value, "section", other_half)
        return jnp.where(upper == 0, value, theirs), jnp.where(upper == 0, theirs, value)

    def rows_of(ids):
        mine = lax.dynamic_slice_in_dim(ids, upper * own_micros, own_micros, 0)
        blocks = [
            lax.dynamic_slice_in_dim(mine, block * tok_rows, tok_rows, 1)
            for block in (expert_id, expert_id ^ 1)
        ]
        return jnp.concatenate([b.reshape(row_count, -1) for b in blocks], axis=0)

    matrices = [w_gate[0, 0], w_up[0, 0], w_down[0, 0]]
    sources = matrices + gather_ring([half for matrix in matrices for half in halves(matrix)], rings)
    small = lax.optimization_barrier((expert_ids[0], norm_gain, router[0], sources[3 + 6]))
    ids = [rows_of(layer) for layer in both_layers(small[0])]
    scales = both_layers(small[1])
    routers = [
        jnp.pad(layer, ((0, 0), (0, lanes - layer.shape[1]))) for layer in both_layers(small[2])
    ]
    entering = lax.dynamic_slice_in_dim(tokens_in, upper * own_micros, own_micros, 0)
    entering = entering.reshape(row_count, width)

    def exchange(value):
        return lax.ppermute(value, "expert", other_core)

    def ring_step(step, state):
        sent, middle, base, back, stored = state
        flags = [(ring_id == step).astype(jnp.int32), my_z, my_core]
        place = jnp.stack(flags + [(ring_id == step - 1).astype(jnp.int32)])
        mine = lax.ppermute(sent, "section", next_ring)
        ahead = load_ahead(place, sources, middle, base, back, stored)
        mine, (weights, ready, stored) = lax.optimization_barrier((mine, ahead))
        other = exchange(mine)
        part, lent = run_first(place, mine, other, scales[0], ids[0], routers[0], weights)
        back = exchange(lent)
        middle, base, lent = run_second(
            place, mine, other, part, back, scales[1], ids[1], routers[1], ready, sources
        )
        back = exchange(lent)
        sent = (base + back.astype(jnp.float32)).astype(jnp.bfloat16)
        return sent, middle, base, back, stored

    blank = jnp.zeros(entering.shape, jnp.float32)
    state = (entering, blank, blank, entering, (blank, blank + 0))
    _, middle, base, back, stored = lax.fori_loop(0, rings, ring_step, state)
    final = ring_id == rings - 1
    stored_first = jnp.where(final, middle, stored[0])
    stored_second = jnp.where(final, base + back.astype(jnp.float32), stored[1])
    kept = jnp.where(upper == 0, stored_first, stored_second)
    given = jnp.where(upper == 0, stored_second, stored_first)
    taken = lax.ppermute(given.astype(jnp.bfloat16), "section", other_half).astype(jnp.float32)
    low = jnp.where(upper == 0, kept, taken)
    high = jnp.where(upper == 0, taken, kept)
    return jnp.concatenate([low, high], axis=0).reshape(1, micro_count, tok_rows, width)


def solution(mesh):
    return jax.shard_map(
        shards,
        mesh=mesh,
        in_specs=(
            P(None, "expert", None),
            P("section", None, None, None),
            P("section", None, None),
            P("section", None),
            P("section", "expert", None, None),
            P("section", "expert", None, None),
            P("section", "expert", None, None),
        ),
        out_specs=P("section", None, "expert", None),
        check_vma=False,
    )
```
